32 devices in a mesh: xy: 8 (over y, x, core), gz: 4 (over z).
Axes of the slice: x: 2, y: 2, z: 4, core: 2. Of those that a mesh axis runs over, the one named last changes fastest.
Arguments:
- electric: float32 [4, 2048, 2048], P('gz', 'xy'), may hold values from -6 to 6
- magnetic_first: float32 [4, 2048, 2048], P('gz', 'xy'), may hold values from -6 to 6
- magnetic_second: float32 [4, 2048, 2048], P('gz', 'xy'), may hold values from -6 to 6
- region: int32 [4, 2048, 2048], P('gz', 'xy'), may hold values from 0 to 7
- permittivity_table: float32 [8], replicated, may hold values from 1 to 12
- conductivity_table: float32 [8], replicated, may hold values from 0.02 to 4
Outputs:
- electric_final: float32 [4, 2048, 2048], P('gz', 'xy')
- first_final: float32 [4, 2048, 2048], P('gz', 'xy')
- second_final: float32 [4, 2048, 2048], P('gz', 'xy')
The draws below stay inside these ranges and needn't reach their ends.
All inputs are finite; a program needn't handle non-finite values.
Results may differ from the reference program's by a relative error of at most 0.000024.
Values sent between devices are 32-bit elements; how exact they have to be, the bound alone decides.
A program may use at most 128 MiB of HBM per device.

```python
import math
import jax
import jax.numpy as jnp
from jax import lax

NX = 2048
NY = 2048
REGIONS = 8
NZ = 4


def plant(drawn, own_key, smallest, top_value):
    place = [jax.random.randint(jax.random.fold_in(own_key, axis), (), 0, length) for axis, length in enumerate(drawn.shape)]
    main_axis = drawn.shape.index(max(drawn.shape))
    beside = place[:main_axis] + [(place[main_axis] + 1) % drawn.shape[main_axis]] + place[main_axis + 1:]
    return drawn.at[tuple(place)].set(smallest).at[tuple(beside)].set(top_value)


def level_of(own_key, extent, split, low, high):
    def one(dim, parts):
        heights = jax.random.uniform(jax.random.fold_in(jax.random.fold_in(own_key, 6), dim), (parts,), jnp.float32, low / len(split), high / len(split))
        return jnp.repeat(jnp.exp(heights), extent[dim] // parts).reshape((-1,) + (1,) * (len(extent) - dim - 1))

    gain = one(*split[0])
    for cut in split[1:]:
        gain = gain * one(*cut)
    return gain


def bell_draw(key, dims, width, bound, shards=(), kind=jnp.bfloat16):
    entries = width * jax.random.normal(key, dims, jnp.float32)
    if shards:
        entries = entries * level_of(key, dims, shards, -0.22, 0.18)
    return jnp.clip(entries, -bound, bound).astype(kind)


def setup_inputs(seed: int = 0) -> dict:
    key_list = jax.random.split(jax.random.key(seed), 7)
    electric = bell_draw(key_list[0], (NZ, NY, NX), 1.0, 6.0, ((0, 4), (1, 8)), jnp.float32)
    magnetic_first = bell_draw(key_list[1], (NZ, NY, NX), 1.0, 6.0, ((0, 4), (1, 8)), jnp.float32)
    magnetic_second = bell_draw(key_list[2], (NZ, NY, NX), 1.0, 6.0, ((0, 4), (1, 8)), jnp.float32)
    region = plant(jax.random.randint(key_list[3], (NZ, NY, NX), 0, REGIONS), jax.random.fold_in(key_list[3], 1), 0, REGIONS - 1).astype(jnp.int32)
    permittivity_table = jnp.clip(jnp.exp(jax.random.uniform(key_list[4], (REGIONS,), jnp.float32, math.log(1.0), math.log(12.0))), 1.0, 12.0)
    conductivity_table = jnp.clip(jnp.exp(jax.random.uniform(key_list[5], (REGIONS,), jnp.float32, math.log(0.02), math.log(4.0))), 0.02, 4.0)
    return dict(electric=electric, magnetic_first=magnetic_first, magnetic_second=magnetic_second, region=region, permittivity_table=permittivity_table, conductivity_table=conductivity_table)


time_step = 4.0
vertical_coupling = 0.5

def neighbour(values, axis, step):
    length = values.shape[axis]
    widths = [(0, 0)] * values.ndim
    if step > 0:
        widths[axis] = (0, step)
        begin = step
    else:
        widths[axis] = (-step, 0)
        begin = 0
    padded = jnp.pad(values, widths)
    return lax.slice_in_dim(padded, begin, begin + length, axis=axis)

def vertical(values):
    return neighbour(values, 0, 1) + neighbour(values, 0, -1) - 2.0 * values

def solve_lines(diagonal, right_side):
    length = diagonal.shape[-1]
    index = jnp.arange(length)
    lower_band = jnp.broadcast_to(jnp.where(index > 0, -time_step, 0.0), diagonal.shape[1:]).astype(diagonal.dtype)
    upper_band = jnp.broadcast_to(jnp.where(index < length - 1, -time_step, 0.0), diagonal.shape[1:]).astype(diagonal.dtype)

    def plane(pair):
        solved = lax.linalg.tridiagonal_solve(lower_band, pair[0], upper_band, pair[1][..., None])
        return solved[..., 0]
    return lax.map(plane, (diagonal, right_side))

def reference(electric, magnetic_first, magnetic_second, region, permittivity_table, conductivity_table):
    rate = time_step
    permittivity = permittivity_table[region]
    conductivity = conductivity_table[region]
    dplus = permittivity / time_step + 0.5 * conductivity
    dminus = permittivity / time_step - 0.5 * conductivity
    rhs_one = dminus * electric + (magnetic_second - neighbour(magnetic_second, 2, -1)) - (magnetic_first - neighbour(magnetic_first, 1, -1)) + vertical_coupling * vertical(electric)
    ramp_x = jnp.where(jnp.arange(NX) > 0, 2.0 * rate, rate)
    half_e = solve_lines(dplus + ramp_x, rhs_one)
    half_hy = magnetic_second + rate * (neighbour(half_e, 2, 1) - half_e)
    half_hx = magnetic_first - rate * (neighbour(electric, 1, 1) - electric)
    rhs_two = dminus * half_e + (half_hy - neighbour(half_hy, 2, -1)) - (half_hx - neighbour(half_hx, 1, -1)) + vertical_coupling * vertical(half_e)
    ramp_y = jnp.where(jnp.arange(NY) > 0, 2.0 * rate, rate)
    swapped_rhs = jnp.transpose(rhs_two, (0, 2, 1))
    swapped_dplus = jnp.transpose(dplus, (0, 2, 1))
    full_e = solve_lines(swapped_dplus + ramp_y, swapped_rhs)
    swapped_hx = jnp.transpose(half_hx, (0, 2, 1))
    full_hx = swapped_hx - rate * (neighbour(full_e, 2, 1) - full_e)
    full_hy = half_hy + rate * (neighbour(half_e, 2, 1) - half_e)
    return (full_e, full_hx, jnp.transpose(full_hy, (0, 2, 1)))
```

```python
import functools

import jax
import jax.numpy as jnp
from jax import lax
from jax.experimental import pallas as pl
from jax.experimental.pallas import tpu as pltpu
from jax.sharding import PartitionSpec as P

time_step = 4.0
vertical_coupling = 0.5
run_length = 32
vmem_bytes = 56 * 1024 * 1024


def passed_along(value, axis, steps):
    count = lax.axis_size(axis)
    initial, last = (max(0, -steps), min(count, count - steps))
    return lax.ppermute(value, axis, [(source, source + steps) for source in range(initial, last)])


def shifted(values, step, axis):
    size = values.shape[axis]
    return pltpu.roll(values, step % size, axis)


def row_index(shape):
    return lax.broadcasted_iota(jnp.int32, shape, 0)


def lookup(region, entries):
    level = list(entries)
    bit = 1
    while len(level) > 1:
        on = (region & bit) != 0
        level = [jnp.where(on, level[i + 1], level[i]) for i in range(0, len(level), 2)]
        bit *= 2
    return level[0]


def cyclic(diagonal, lower, upper, right_side):
    count = diagonal.shape[0]
    stride = 1
    while stride < count:
        inverse = 1.0 / diagonal
        alpha = lower * shifted(inverse, stride, 0)
        beta = upper * shifted(inverse, -stride, 0)
        diagonal = (
            diagonal
            - alpha * shifted(upper, stride, 0)
            - beta * shifted(lower, -stride, 0)
        )
        right_side = (
            right_side
            + alpha * shifted(right_side, stride, 0)
            + beta * shifted(right_side, -stride, 0)
        )
        lower = alpha * shifted(lower, stride, 0)
        upper = beta * shifted(upper, -stride, 0)
        stride *= 2
    return right_side / diagonal


def run_rows(ref, step, runs, length):
    return ref[pl.ds(step, runs, stride=length), :]


def run_blocks(ref, blocks, step, runs, length):
    return jnp.concatenate(
        [ref[block, pl.ds(step, runs, stride=length), :] for block in blocks], axis=1
    )


def eliminate(diagonal_of, right_of, runs, length, c_ref, g_ref, f_ref):
    c = g = f = total_g = total_f = None
    for i in range(length - 1):
        d, b = diagonal_of(i), right_of(i)
        if i == 0:
            inverse = 1.0 / d
            c = time_step * inverse
            g = b * inverse
            f = c
            total_g, total_f = g, f
        else:
            inverse = 1.0 / (d - time_step * c)
            c = time_step * inverse
            g = (b + time_step * g) * inverse
            before = f
            f = c * f
            total_g = total_g + before * g
            total_f = total_f + before * f
        rows = pl.ds(i * runs, runs)
        c_ref[rows, :] = c
        g_ref[rows, :] = g
        f_ref[rows, :] = f
    d, b = diagonal_of(length - 1), right_of(length - 1)
    return (
        d - time_step * c,
        b + time_step * g,
        time_step * f,
        time_step * total_g,
        time_step * total_f,
    )


def back(last, before, runs, length, c_ref, g_ref, f_ref, put):
    x = last
    put(length - 1, x)
    for i in range(length - 2, -1, -1):
        rows = pl.ds(i * runs, runs)
        x = g_ref[rows, :] + c_ref[rows, :] * x + f_ref[rows, :] * before
        put(i, x)


def table_entries(eps_ref, sig_ref):
    eps = [eps_ref[k] / time_step for k in range(eps_ref.shape[0])]
    sig = [0.5 * sig_ref[k] for k in range(sig_ref.shape[0])]
    return [a + b for a, b in zip(eps, sig)], [a - b for a, b in zip(eps, sig)]


def column_block(block, parts):
    return block % parts, slice((block // parts) * 128, (block // parts) * 128 + 128)


def x_kernel(parts, e_ref, up_ref, down_ref, hx_ref, hx_edge_ref, hy_ref, region_ref,
             eps_ref, sig_ref, *rest):
    outs, (rhs, dia, rhs_t, dia_t, c_ref, g_ref, f_ref) = rest[:parts], rest[parts:]
    rows, columns = e_ref.shape
    plus, minus = table_entries(eps_ref, sig_ref)
    for first in range(0, rows, 8):
        here = pl.ds(first, 8)
        e, hx, hy, region = e_ref[here, :], hx_ref[here, :], hy_ref[here, :], region_ref[here, :]
        column = lax.broadcasted_iota(jnp.int32, e.shape, 1)
        edge = hx_edge_ref[0:1, :] if first == 0 else hx_ref[first - 1:first, :]
        hx_before = jnp.where(row_index(e.shape) == 0, edge, shifted(hx, 1, 0))
        hy_before = jnp.where(column == 0, 0.0, shifted(hy, 1, 1))
        layer = up_ref[here, :] + down_ref[here, :] - 2.0 * e
        rhs[here, :] = (
            lookup(region, minus) * e
            + (hy - hy_before)
            - (hx - hx_before)
            + vertical_coupling * layer
        )
        dia[here, :] = lookup(region, plus) + jnp.where(column == 0, time_step, 2.0 * time_step)
    if rhs.shape[0] > rows:
        rest_shape = (rhs.shape[0] - rows, columns)
        rhs[rows:, :] = jnp.zeros(rest_shape, jnp.float32)
        dia[rows:, :] = jnp.full(rest_shape, 3.0 * time_step, jnp.float32)
    for start in range(0, columns, 128):
        rhs_t[start:start + 128, :] = rhs[:, start:start + 128].T
        dia_t[start:start + 128, :] = dia[:, start:start + 128].T
    runs, length = columns // run_length, run_length
    d, b, off, part_g, part_f = eliminate(
        lambda i: run_rows(dia_t, i, runs, length),
        lambda i: run_rows(rhs_t, i, runs, length),
        runs, length, c_ref, g_ref, f_ref,
    )
    place = row_index(d.shape)
    off = jnp.where(place == 0, 0.0, off)
    end = place == runs - 1
    d = d - jnp.where(end, 0.0, shifted(part_f, -1, 0))
    b = b + jnp.where(end, 0.0, shifted(part_g, -1, 0))
    solved = cyclic(d, off, jnp.where(end, 0.0, shifted(off, -1, 0)), b)
    before = jnp.where(place == 0, 0.0, shifted(solved, 1, 0))

    def put(i, x):
        rhs_t[pl.ds(i, runs, stride=length), :] = x

    back(solved, before, runs, length, c_ref, g_ref, f_ref, put)
    for block in range(columns // 128):
        part, place = column_block(block, parts)
        outs[part][:, place] = rhs_t[block * 128:block * 128 + 128, :].T[:rows]


def middle_kernel(parts, pieces, first_ref, e_ref, hx_ref, hy_ref, region_ref, e_before_ref,
                  e_after_ref, hx_edge_ref, eps_ref, sig_ref, *rest):
    halves = rest[:parts * pieces]
    rhs_outs = rest[parts * pieces:parts * pieces + parts]
    dia_outs = rest[parts * pieces + parts:parts * pieces + 2 * parts]
    hx_outs = rest[parts * pieces + 2 * parts:parts * pieces + 3 * parts]
    hy_out, half_ref, full_ref = rest[parts * pieces + 3 * parts:]
    rows, columns = e_ref.shape
    piece_rows = rows // pieces
    blocks = columns // 128
    for piece in range(pieces):
        for block in range(blocks):
            part, place = column_block(block, parts)
            half_ref[piece * piece_rows:(piece + 1) * piece_rows, block * 128:block * 128 + 128] = (
                halves[piece * parts + part][:, place]
            )
    plus, minus = table_entries(eps_ref, sig_ref)
    edge_before = hx_edge_ref[0:1, :] - time_step * (e_ref[0:1, :] - e_before_ref[0:1, :])
    edge_before = jnp.where(first_ref[0] > 0, 0.0, edge_before)
    for first in range(0, rows, 8):
        here = pl.ds(first, 8)
        e, hx, hy, region = e_ref[here, :], hx_ref[here, :], hy_ref[here, :], region_ref[here, :]
        half = half_ref[here, :]
        place = row_index(e.shape)
        column = lax.broadcasted_iota(jnp.int32, e.shape, 1)
        after = e_after_ref[0:1, :] if first + 8 == rows else e_ref[first + 8:first + 9, :]
        e_after = jnp.where(place == 7, after, shifted(e, -1, 0))
        half_hx = hx - time_step * (e_after - e)
        hx_before = jnp.where(place == 0, edge_before, shifted(half_hx, 1, 0))
        edge_before = half_hx[7:8, :]
        half_after = jnp.where(column == columns - 1, 0.0, shifted(half, -1, 1))
        change = time_step * (half_after - half)
        half_hy = hy + change
        full_ref[here, :] = half_hy + change
        hy_before = jnp.where(column == 0, 0.0, shifted(half_hy, 1, 1))
        right_side = (
            lookup(region, minus) * half
            + (half_hy - hy_before)
            - (half_hx - hx_before)
            - (2.0 * vertical_coupling) * half
        )
        ramp = 2.0 * time_step
        diagonal = lookup(region, plus) + ramp
        if first == 0:
            start = jnp.where(first_ref[0] > 0, time_step, 2.0 * time_step)
            diagonal = lookup(region, plus) + jnp.where(place == 0, start, ramp)
        for block in range(blocks):
            part, spot = column_block(block, parts)
            source = slice(block * 128, block * 128 + 128)
            rhs_outs[part][here, spot] = right_side[:, source]
            dia_outs[part][spot.start // 128, here, :] = diagonal[:, source]
            hx_outs[part][here, spot] = half_hx[:, source]
    for block in range(blocks):
        hy_out[block * 128:block * 128 + 128, :] = full_ref[:, block * 128:block * 128 + 128].T


def y_first_kernel(pieces, runs, rhs_ref, dia_ref, *rest):
    ups, downs = rest[:pieces], rest[pieces:2 * pieces]
    c_ref, g_ref, f_ref, second_ref, sent_ref, total = rest[2 * pieces:]
    rows, columns = rhs_ref.shape
    piece_rows = rows // pieces
    for piece in range(pieces):
        here = slice(piece * piece_rows, (piece + 1) * piece_rows)
        for block in range(columns // 128):
            spot = slice(block * 128, block * 128 + 128)
            total[block, here, :] = rhs_ref[here, spot] + vertical_coupling * (
                ups[piece][:, spot] + downs[piece][:, spot]
            )
    length = rows // runs
    for start in range(0, columns, 512):
        some = pl.ds(start, 512)
        blocks = range(start // 128, start // 128 + 4)
        d, b, off, part_g, part_f = eliminate(
            lambda i: run_blocks(dia_ref, blocks, i, runs, length),
            lambda i: run_blocks(total, blocks, i, runs, length),
            runs, length, c_ref.at[:, some], g_ref.at[:, some], f_ref.at[:, some],
        )
        end = row_index(d.shape) == runs - 1
        d = d - jnp.where(end, 0.0, shifted(part_f, -1, 0))
        b = b + jnp.where(end, 0.0, shifted(part_g, -1, 0))
        coupling = [off[k:k + 1, :] for k in range(runs)]
        c = g = f = total_g = total_f = factor = None
        for k in range(runs - 1):
            if k == 0:
                inverse = 1.0 / d[0:1, :]
                c = coupling[1] * inverse
                g = b[0:1, :] * inverse
                f = coupling[0] * inverse
                total_g, total_f, factor = g, f, c
            else:
                inverse = 1.0 / (d[k:k + 1, :] - coupling[k] * c)
                c = coupling[k + 1] * inverse
                g = (b[k:k + 1, :] + coupling[k] * g) * inverse
                f = coupling[k] * f * inverse
                total_g = total_g + factor * g
                total_f = total_f + factor * f
                factor = factor * c
            second_ref[k:k + 1, some] = c
            second_ref[runs + k:runs + k + 1, some] = g
            second_ref[2 * runs + k:2 * runs + k + 1, some] = f
        sent_ref[0:1, some] = d[runs - 1:runs, :] - coupling[runs - 1] * c
        sent_ref[1:2, some] = b[runs - 1:runs, :] + coupling[runs - 1] * g
        sent_ref[2:3, some] = coupling[runs - 1] * f
        sent_ref[3:4, some] = part_g[0:1, :] + coupling[0] * total_g
        sent_ref[4:5, some] = part_f[0:1, :] + coupling[0] * total_f
        sent_ref[5:8, some] = jnp.zeros((3, 512), jnp.float32)


def y_second_kernel(count, runs, me_ref, all_ref, c_ref, g_ref, f_ref, second_ref, hx_ref,
                    e_out, hx_out, e_scr, hx_scr, solved_scr):
    rows, columns = hx_ref.shape
    length = rows // runs
    me = me_ref[0]
    for start in range(0, columns, 512):
        some = pl.ds(start, 512)
        blocks = range(start // 128, start // 128 + 4)
        d, b, off, part_g, part_f = [
            all_ref[q, :, some] for q in range(5)
        ]
        place = row_index(d.shape)
        end = place == count - 1
        off = jnp.where(place == 0, 0.0, off)
        off_next = jnp.where(end, 0.0, shifted(off, -1, 0))
        f_next = jnp.where(end, 0.0, shifted(part_f, -1, 0))
        g_next = jnp.where(end, 0.0, shifted(part_g, -1, 0))
        solved = cyclic(d - f_next, off, off_next, b + g_next)
        next_row = (
            g_next
            + f_next * solved
            + off_next * jnp.where(end, 0.0, shifted(solved, -1, 0))
        ) / time_step

        def row_of(values, index):
            return jnp.sum(jnp.where(place == index, values, 0.0), axis=0, keepdims=True)

        own, previous = row_of(solved, me), row_of(solved, me - 1)
        beyond = row_of(next_row, me)
        value = own
        solved_scr[runs - 1:runs, some] = own
        for k in range(runs - 2, -1, -1):
            value = (
                second_ref[runs + k:runs + k + 1, some]
                + second_ref[k:k + 1, some] * value
                + second_ref[2 * runs + k:2 * runs + k + 1, some] * previous
            )
            solved_scr[k:k + 1, some] = value
        last = solved_scr[:, some]
        before = jnp.where(row_index(last.shape) == 0, previous, shifted(last, 1, 0))

        def put(i, x):
            for n, block in enumerate(blocks):
                e_scr[block, pl.ds(i, runs, stride=length), :] = x[:, n * 128:n * 128 + 128]

        back(last, before, runs, length, c_ref.at[:, some], g_ref.at[:, some],
             f_ref.at[:, some], put)
        for first in range(0, rows, 8):
            here = pl.ds(first, 8)
            e = jnp.concatenate([e_scr[n, here, :] for n in blocks], axis=1)
            after = beyond
            if first + 8 < rows:
                after = jnp.concatenate(
                    [e_scr[n, first + 8:first + 9, :] for n in blocks], axis=1
                )
            e_after = jnp.where(row_index(e.shape) == 7, after, shifted(e, -1, 0))
            hx_scr[here, some] = hx_ref[here, some] - time_step * (e_after - e)
    for start in range(0, columns, 128):
        block = slice(start, start + 128)
        e_out[block, :] = e_scr[start // 128].T
        hx_out[block, :] = hx_scr[:, block].T


in_vmem = pl.BlockSpec(memory_space=pltpu.VMEM)
in_smem = pl.BlockSpec(memory_space=pltpu.SMEM)


def called(kernel, outs, scratch, specs, values, operands):
    return pl.pallas_call(
        kernel,
        out_shape=[jax.ShapeDtypeStruct(shape, jnp.float32) for shape in outs],
        in_specs=specs,
        out_specs=[in_vmem] * len(outs),
        scratch_shapes=[pltpu.VMEM(shape, jnp.float32) for shape in scratch],
        compiler_params=pltpu.CompilerParams(vmem_limit_bytes=vmem_bytes),
        cost_estimate=pl.CostEstimate(
            flops=40 * values, bytes_accessed=30 * values, transcendentals=0
        ),
    )(*operands)


def local(
    electric, magnetic_first, magnetic_second, region, permittivity_table, conductivity_table
):
    count = lax.axis_size("xy")
    me = lax.axis_index("xy")
    _, rows, columns = electric.shape
    width = columns // count
    pieces = 2 if rows % 256 == 0 else 1
    parts = 2 if width == 256 else 1
    piece_rows = rows // pieces
    part_columns = columns // parts
    runs = 8
    electric, hx, hy, region = (
        v.reshape(rows, columns) for v in (electric, magnetic_first, magnetic_second, region)
    )
    eps, sig = permittivity_table, conductivity_table
    first_flag = (me == 0).astype(jnp.int32).reshape(1)
    me_value = me.astype(jnp.int32).reshape(1)

    cut = [slice(p * piece_rows, (p + 1) * piece_rows) for p in range(pieces)]
    ups = [passed_along(electric[c], "gz", 1) for c in cut]
    downs = [passed_along(electric[c], "gz", -1) for c in cut]
    hx_edge = passed_along(hx[-1:], "xy", 1)
    e_before = passed_along(electric[-1:], "xy", 1)
    e_after = passed_along(electric[:1], "xy", -1)

    halves = []
    lines = max(piece_rows, 128)
    t_shape = (columns, lines)
    for p in range(pieces):
        edge = hx_edge if p == 0 else hx[p * piece_rows - 1:p * piece_rows]
        halves.append(called(
            functools.partial(x_kernel, parts),
            [(piece_rows, part_columns)] * parts,
            [(lines, columns)] * 2 + [t_shape] * 2 + [((run_length - 1) * columns // run_length, lines)] * 3,
            [in_vmem] * 7 + [in_smem] * 2,
            piece_rows * columns,
            (electric[cut[p]], ups[p], downs[p], hx[cut[p]], edge, hy[cut[p]], region[cut[p]],
             eps, sig),
        ))
    half_up = [[passed_along(halves[p][c], "gz", 1) for p in range(pieces)] for c in range(parts)]
    half_down = [
        [passed_along(halves[p][c], "gz", -1) for p in range(pieces)] for c in range(parts)
    ]
    middle = called(
        functools.partial(middle_kernel, parts, pieces),
        [(rows, part_columns)] * parts
        + [(part_columns // 128, rows, 128)] * parts
        + [(rows, part_columns)] * parts
        + [(columns, rows)],
        [(rows, columns)] * 2,
        [in_smem] + [in_vmem] * 7 + [in_smem] * 2 + [in_vmem] * (parts * pieces),
        rows * columns,
        (first_flag, electric, hx, hy, region, e_before, e_after, hx_edge, eps, sig,
         *[halves[p][c] for p in range(pieces) for c in range(parts)]),
    )
    right_sides, diagonals = middle[:parts], middle[parts:2 * parts]
    half_hx, full_hy_t = middle[2 * parts:3 * parts], middle[3 * parts]

    def exchanged(values, size):
        moved = lax.all_to_all(
            values.reshape(count, size, rows), "xy", split_axis=0, concat_axis=0, tiled=True
        )
        return moved

    def joined(moved):
        return jnp.transpose(moved, (1, 0, 2)).reshape(1, moved.shape[1], count * rows)

    full_hy = joined(exchanged(full_hy_t, width))
    pairs = []
    for c in range(parts):
        length = rows // runs
        kept = ((length - 1) * runs, part_columns)
        firsts = called(
            functools.partial(y_first_kernel, pieces, runs),
            [kept] * 3 + [(3 * runs, part_columns), (8, part_columns)],
            [(part_columns // 128, rows, 128)],
            [in_vmem] * (2 + 2 * pieces),
            rows * part_columns,
            (right_sides[c], diagonals[c], *half_up[c], *half_down[c]),
        )
        everyone = jnp.swapaxes(lax.all_gather(firsts[4], "xy"), 0, 1)
        seconds = called(
            functools.partial(y_second_kernel, count, runs),
            [(part_columns, rows)] * 2,
            [(part_columns // 128, rows, 128), (rows, part_columns), (runs, part_columns)],
            [in_smem] + [in_vmem] * 6,
            rows * part_columns,
            (me_value, everyone, *firsts[:4], half_hx[c]),
        )
        pairs.append([exchanged(v, width // parts) for v in seconds])
    full_e, full_hx = (
        joined(jnp.concatenate([pair[q] for pair in pairs], axis=1)) for q in range(2)
    )
    return (full_e, full_hx, full_hy)


def solution(mesh):
    in_specs = (
        P("gz", "xy", None),
        P("gz", "xy", None),
        P("gz", "xy", None),
        P("gz", "xy", None),
        P(),
        P(),
    )
    out_specs = (P("gz", "xy", None), P("gz", "xy", None), P("gz", "xy", None))
    return jax.shard_map(local, mesh=mesh, in_specs=in_specs, out_specs=out_specs, check_vma=False)
```

```python
import functools

import jax
import jax.numpy as jnp
from jax import lax
from jax.experimental import pallas as pl
from jax.experimental.pallas import tpu as pltpu
from jax.sharding import PartitionSpec as P

time_step = 4.0
vertical_coupling = 0.5
run_length = 32
vmem_bytes = 56 * 1024 * 1024


def passed_along(value, axis, steps):
    count = lax.axis_size(axis)
    initial, last = (max(0, -steps), min(count, count - steps))
    return lax.ppermute(value, axis, [(source, source + steps) for source in range(initial, last)])


def shifted(values, step, axis):
    size = values.shape[axis]
    return pltpu.roll(values, step % size, axis)


def row_index(shape):
    return lax.broadcasted_iota(jnp.int32, shape, 0)


def lookup(region, entries):
    level = list(entries)
    bit = 1
    while len(level) > 1:
        on = (region & bit) != 0
        level = [jnp.where(on, level[i + 1], level[i]) for i in range(0, len(level), 2)]
        bit *= 2
    return level[0]


def cyclic(diagonal, lower, upper, right_side):
    count = diagonal.shape[0]
    stride = 1
    while stride < count:
        inverse = 1.0 / diagonal
        alpha = lower * shifted(inverse, stride, 0)
        beta = upper * shifted(inverse, -stride, 0)
        diagonal = (
            diagonal
            - alpha * shifted(upper, stride, 0)
            - beta * shifted(lower, -stride, 0)
        )
        right_side = (
            right_side
            + alpha * shifted(right_side, stride, 0)
            + beta * shifted(right_side, -stride, 0)
        )
        lower = alpha * shifted(lower, stride, 0)
        upper = beta * shifted(upper, -stride, 0)
        stride *= 2
    return right_side / diagonal


def run_rows(ref, step, runs, length):
    return ref[pl.ds(step, runs, stride=length), :]


def run_blocks(ref, blocks, step, runs, length):
    return jnp.concatenate(
        [ref[block, pl.ds(step, runs, stride=length), :] for block in blocks], axis=1
    )


def eliminate(diagonal_of, right_of, runs, length, c_ref, g_ref, f_ref):
    c = g = f = total_g = total_f = None
    for i in range(length - 1):
        d, b = diagonal_of(i), right_of(i)
        if i == 0:
            inverse = 1.0 / d
            c = time_step * inverse
            g = b * inverse
            f = c
            total_g, total_f = g, f
        else:
            inverse = 1.0 / (d - time_step * c)
            c = time_step * inverse
            g = (b + time_step * g) * inverse
            before = f
            f = c * f
            total_g = total_g + before * g
            total_f = total_f + before * f
        rows = pl.ds(i * runs, runs)
        c_ref[rows, :] = c
        g_ref[rows, :] = g
        f_ref[rows, :] = f
    d, b = diagonal_of(length - 1), right_of(length - 1)
    return (
        d - time_step * c,
        b + time_step * g,
        time_step * f,
        time_step * total_g,
        time_step * total_f,
    )


def back(last, before, runs, length, c_ref, g_ref, f_ref, put):
    x = last
    put(length - 1, x)
    for i in range(length - 2, -1, -1):
        rows = pl.ds(i * runs, runs)
        x = g_ref[rows, :] + c_ref[rows, :] * x + f_ref[rows, :] * before
        put(i, x)


def table_entries(eps_ref, sig_ref):
    eps = [eps_ref[k] / time_step for k in range(eps_ref.shape[0])]
    sig = [0.5 * sig_ref[k] for k in range(sig_ref.shape[0])]
    return [a + b for a, b in zip(eps, sig)], [a - b for a, b in zip(eps, sig)]


def column_block(block, parts):
    return block % parts, slice((block // parts) * 128, (block // parts) * 128 + 128)


def x_kernel(parts, e_ref, up_ref, down_ref, hx_ref, hx_edge_ref, hy_ref, region_ref,
             eps_ref, sig_ref, *rest):
    outs, (rhs, dia, rhs_t, dia_t, c_ref, g_ref, f_ref) = rest[:parts], rest[parts:]
    rows, columns = e_ref.shape
    plus, minus = table_entries(eps_ref, sig_ref)
    for first in range(0, rows, 8):
        here = pl.ds(first, 8)
        e, hx, hy, region = e_ref[here, :], hx_ref[here, :], hy_ref[here, :], region_ref[here, :]
        column = lax.broadcasted_iota(jnp.int32, e.shape, 1)
        edge = hx_edge_ref[0:1, :] if first == 0 else hx_ref[first - 1:first, :]
        hx_before = jnp.where(row_index(e.shape) == 0, edge, shifted(hx, 1, 0))
        hy_before = jnp.where(column == 0, 0.0, shifted(hy, 1, 1))
        layer = up_ref[here, :] + down_ref[here, :] - 2.0 * e
        rhs[here, :] = (
            lookup(region, minus) * e
            + (hy - hy_before)
            - (hx - hx_before)
            + vertical_coupling * layer
        )
        dia[here, :] = lookup(region, plus) + jnp.where(column == 0, time_step, 2.0 * time_step)
    if rhs.shape[0] > rows:
        rest_shape = (rhs.shape[0] - rows, columns)
        rhs[rows:, :] = jnp.zeros(rest_shape, jnp.float32)
        dia[rows:, :] = jnp.full(rest_shape, 3.0 * time_step, jnp.float32)
    for start in range(0, columns, 128):
        rhs_t[start:start + 128, :] = rhs[:, start:start + 128].T
        dia_t[start:start + 128, :] = dia[:, start:start + 128].T
    runs, length = columns // run_length, run_length
    d, b, off, part_g, part_f = eliminate(
        lambda i: run_rows(dia_t, i, runs, length),
        lambda i: run_rows(rhs_t, i, runs, length),
        runs, length, c_ref, g_ref, f_ref,
    )
    place = row_index(d.shape)
    off = jnp.where(place == 0, 0.0, off)
    end = place == runs - 1
    d = d - jnp.where(end, 0.0, shifted(part_f, -1, 0))
    b = b + jnp.where(end, 0.0, shifted(part_g, -1, 0))
    solved = cyclic(d, off, jnp.where(end, 0.0, shifted(off, -1, 0)), b)
    before = jnp.where(place == 0, 0.0, shifted(solved, 1, 0))

    def put(i, x):
        rhs_t[pl.ds(i, runs, stride=length), :] = x

    back(solved, before, runs, length, c_ref, g_ref, f_ref, put)
    for block in range(columns // 128):
        part, place = column_block(block, parts)
        outs[part][:, place] = rhs_t[block * 128:block * 128 + 128, :].T[:rows]


def middle_kernel(parts, pieces, first_ref, e_ref, hx_ref, hy_ref, region_ref, e_before_ref,
                  e_after_ref, hx_edge_ref, eps_ref, sig_ref, *rest):
    halves = rest[:parts * pieces]
    rhs_outs = rest[parts * pieces:parts * pieces + parts]
    dia_outs = rest[parts * pieces + parts:parts * pieces + 2 * parts]
    hx_outs = rest[parts * pieces + 2 * parts:parts * pieces + 3 * parts]
    hy_out, half_ref, full_ref = rest[parts * pieces + 3 * parts:]
    rows, columns = e_ref.shape
    piece_rows = rows // pieces
    blocks = columns // 128
    for piece in range(pieces):
        for block in range(blocks):
            part, place = column_block(block, parts)
            half_ref[piece * piece_rows:(piece + 1) * piece_rows, block * 128:block * 128 + 128] = (
                halves[piece * parts + part][:, place]
            )
    plus, minus = table_entries(eps_ref, sig_ref)
    edge_before = hx_edge_ref[0:1, :] - time_step * (e_ref[0:1, :] - e_before_ref[0:1, :])
    edge_before = jnp.where(first_ref[0] > 0, 0.0, edge_before)
    for first in range(0, rows, 8):
        here = pl.ds(first, 8)
        e, hx, hy, region = e_ref[here, :], hx_ref[here, :], hy_ref[here, :], region_ref[here, :]
        half = half_ref[here, :]
        place = row_index(e.shape)
        column = lax.broadcasted_iota(jnp.int32, e.shape, 1)
        after = e_after_ref[0:1, :] if first + 8 == rows else e_ref[first + 8:first + 9, :]
        e_after = jnp.where(place == 7, after, shifted(e, -1, 0))
        half_hx = hx - time_step * (e_after - e)
        hx_before = jnp.where(place == 0, edge_before, shifted(half_hx, 1, 0))
        edge_before = half_hx[7:8, :]
        half_after = jnp.where(column == columns - 1, 0.0, shifted(half, -1, 1))
        change = time_step * (half_after - half)
        half_hy = hy + change
        full_ref[here, :] = half_hy + change
        hy_before = jnp.where(column == 0, 0.0, shifted(half_hy, 1, 1))
        right_side = (
            lookup(region, minus) * half
            + (half_hy - hy_before)
            - (half_hx - hx_before)
            - (2.0 * vertical_coupling) * half
        )
        ramp = 2.0 * time_step
        diagonal = lookup(region, plus) + ramp
        if first == 0:
            start = jnp.where(first_ref[0] > 0, time_step, 2.0 * time_step)
            diagonal = lookup(region, plus) + jnp.where(place == 0, start, ramp)
        for block in range(blocks):
            part, spot = column_block(block, parts)
            source = slice(block * 128, block * 128 + 128)
            rhs_outs[part][here, spot] = right_side[:, source]
            dia_outs[part][spot.start // 128, here, :] = diagonal[:, source]
            hx_outs[part][here, spot] = half_hx[:, source]
    for block in range(blocks):
        hy_out[block * 128:block * 128 + 128, :] = full_ref[:, block * 128:block * 128 + 128].T


def y_first_kernel(pieces, runs, rhs_ref, dia_ref, *rest):
    ups, downs = rest[:pieces], rest[pieces:2 * pieces]
    c_ref, g_ref, f_ref, second_ref, sent_ref, total = rest[2 * pieces:]
    rows, columns = rhs_ref.shape
    piece_rows = rows // pieces
    for piece in range(pieces):
        here = slice(piece * piece_rows, (piece + 1) * piece_rows)
        for block in range(columns // 128):
            spot = slice(block * 128, block * 128 + 128)
            total[block, here, :] = rhs_ref[here, spot] + vertical_coupling * (
                ups[piece][:, spot] + downs[piece][:, spot]
            )
    length = rows // runs
    for start in range(0, columns, 512):
        some = pl.ds(start, 512)
        blocks = range(start // 128, start // 128 + 4)
        d, b, off, part_g, part_f = eliminate(
            lambda i: run_blocks(dia_ref, blocks, i, runs, length),
            lambda i: run_blocks(total, blocks, i, runs, length),
            runs, length, c_ref.at[:, some], g_ref.at[:, some], f_ref.at[:, some],
        )
        end = row_index(d.shape) == runs - 1
        d = d - jnp.where(end, 0.0, shifted(part_f, -1, 0))
        b = b + jnp.where(end, 0.0, shifted(part_g, -1, 0))
        coupling = [off[k:k + 1, :] for k in range(runs)]
        c = g = f = total_g = total_f = factor = None
        for k in range(runs - 1):
            if k == 0:
                inverse = 1.0 / d[0:1, :]
                c = coupling[1] * inverse
                g = b[0:1, :] * inverse
                f = coupling[0] * inverse
                total_g, total_f, factor = g, f, c
            else:
                inverse = 1.0 / (d[k:k + 1, :] - coupling[k] * c)
                c = coupling[k + 1] * inverse
                g = (b[k:k + 1, :] + coupling[k] * g) * inverse
                f = coupling[k] * f * inverse
                total_g = total_g + factor * g
                total_f = total_f + factor * f
                factor = factor * c
            second_ref[k:k + 1, some] = c
            second_ref[runs + k:runs + k + 1, some] = g
            second_ref[2 * runs + k:2 * runs + k + 1, some] = f
        sent_ref[0:1, some] = d[runs - 1:runs, :] - coupling[runs - 1] * c
        sent_ref[1:2, some] = b[runs - 1:runs, :] + coupling[runs - 1] * g
        sent_ref[2:3, some] = coupling[runs - 1] * f
        sent_ref[3:4, some] = part_g[0:1, :] + coupling[0] * total_g
        sent_ref[4:5, some] = part_f[0:1, :] + coupling[0] * total_f
        sent_ref[5:8, some] = jnp.zeros((3, 512), jnp.float32)


def y_second_kernel(count, runs, me_ref, all_ref, c_ref, g_ref, f_ref, second_ref, hx_ref,
                    e_out, hx_out, e_scr, hx_scr, solved_scr):
    rows, columns = hx_ref.shape
    length = rows // runs
    me = me_ref[0]
    for start in range(0, columns, 512):
        some = pl.ds(start, 512)
        blocks = range(start // 128, start // 128 + 4)
        d, b, off, part_g, part_f = [
            all_ref[q, :, some] for q in range(5)
        ]
        place = row_index(d.shape)
        end = place == count - 1
        off = jnp.where(place == 0, 0.0, off)
        off_next = jnp.where(end, 0.0, shifted(off, -1, 0))
        f_next = jnp.where(end, 0.0, shifted(part_f, -1, 0))
        g_next = jnp.where(end, 0.0, shifted(part_g, -1, 0))
        solved = cyclic(d - f_next, off, off_next, b + g_next)
        next_row = (
            g_next
            + f_next * solved
            + off_next * jnp.where(end, 0.0, shifted(solved, -1, 0))
        ) / time_step

        def row_of(values, index):
            return jnp.sum(jnp.where(place == index, values, 0.0), axis=0, keepdims=True)

        own, previous = row_of(solved, me), row_of(solved, me - 1)
        beyond = row_of(next_row, me)
        value = own
        solved_scr[runs - 1:runs, some] = own
        for k in range(runs - 2, -1, -1):
            value = (
                second_ref[runs + k:runs + k + 1, some]
                + second_ref[k:k + 1, some] * value
                + second_ref[2 * runs + k:2 * runs + k + 1, some] * previous
            )
            solved_scr[k:k + 1, some] = value
        last = solved_scr[:, some]
        before = jnp.where(row_index(last.shape) == 0, previous, shifted(last, 1, 0))

        def put(i, x):
            for n, block in enumerate(blocks):
                e_scr[block, pl.ds(i, runs, stride=length), :] = x[:, n * 128:n * 128 + 128]

        back(last, before, runs, length, c_ref.at[:, some], g_ref.at[:, some],
             f_ref.at[:, some], put)
        for first in range(0, rows, 8):
            here = pl.ds(first, 8)
            e = jnp.concatenate([e_scr[n, here, :] for n in blocks], axis=1)
            after = beyond
            if first + 8 < rows:
                after = jnp.concatenate(
                    [e_scr[n, first + 8:first + 9, :] for n in blocks], axis=1
                )
            e_after = jnp.where(row_index(e.shape) == 7, after, shifted(e, -1, 0))
            hx_scr[here, some] = hx_ref[here, some] - time_step * (e_after - e)
    for start in range(0, columns, 128):
        block = slice(start, start + 128)
        e_out[block, :] = e_scr[start // 128].T
        hx_out[block, :] = hx_scr[:, block].T


in_vmem = pl.BlockSpec(memory_space=pltpu.VMEM)
in_smem = pl.BlockSpec(memory_space=pltpu.SMEM)


def called(kernel, outs, scratch, specs, values, operands):
    return pl.pallas_call(
        kernel,
        out_shape=[jax.ShapeDtypeStruct(shape, jnp.float32) for shape in outs],
        in_specs=specs,
        out_specs=[in_vmem] * len(outs),
        scratch_shapes=[pltpu.VMEM(shape, jnp.float32) for shape in scratch],
        compiler_params=pltpu.CompilerParams(vmem_limit_bytes=vmem_bytes),
        cost_estimate=pl.CostEstimate(
            flops=40 * values, bytes_accessed=30 * values, transcendentals=0
        ),
    )(*operands)


def greet(count, me):
    barrier = pltpu.get_barrier_semaphore()
    for step in range(1, count):
        pl.semaphore_signal(
            barrier, inc=1, device_id={"xy": lax.rem(me + step, count)},
            device_id_type=pl.DeviceIdType.MESH,
        )
    pl.semaphore_wait(barrier, count - 1)


def spread_kernel(count, arrays, *refs):
    sources, outs = refs[:arrays], refs[arrays:2 * arrays]
    send_sems, recv_sems, own_sems = refs[2 * arrays:]
    me = lax.axis_index("xy")
    height, width = outs[0].shape[0], sources[0].shape[1]

    def rows_of(device):
        return pl.ds(pl.multiple_of(device * height, height), height)

    def columns_of(device):
        return pl.ds(pl.multiple_of(device * width, width), width)

    greet(count, me)
    owns, copies = [], []
    for step in range(1, count):
        peer = lax.rem(me + step, count)
        for k in range(arrays):
            copy = pltpu.make_async_remote_copy(
                src_ref=sources[k].at[rows_of(peer), :],
                dst_ref=outs[k].at[:, columns_of(me)],
                send_sem=send_sems.at[k, step - 1],
                recv_sem=recv_sems.at[k, step - 1],
                device_id={"xy": peer},
                device_id_type=pl.DeviceIdType.MESH,
            )
            copy.start()
            copies.append(copy)
    for k in range(arrays):
        own = pltpu.make_async_copy(
            sources[k].at[rows_of(me), :], outs[k].at[:, columns_of(me)], own_sems.at[k]
        )
        own.start()
        owns.append(own)
    for own in owns:
        own.wait()
    for copy in copies:
        copy.wait()


def spread(values, count, number):
    columns, rows = values[0].shape
    anywhere = pl.BlockSpec(memory_space=pl.ANY)
    arrays = len(values)
    sems = pltpu.SemaphoreType.DMA((arrays, count - 1))
    return pl.pallas_call(
        functools.partial(spread_kernel, count, arrays),
        out_shape=[jax.ShapeDtypeStruct((columns // count, rows * count), jnp.float32)] * arrays,
        in_specs=[anywhere] * arrays,
        out_specs=[anywhere] * arrays,
        scratch_shapes=[sems, sems, pltpu.SemaphoreType.DMA((arrays,))],
        compiler_params=pltpu.CompilerParams(collective_id=number, has_side_effects=True),
        cost_estimate=pl.CostEstimate(
            flops=0, bytes_accessed=32 * arrays * rows * columns, transcendentals=0
        ),
    )(*values)


def gather_kernel(count, source, out, send_sems, recv_sems):
    me = lax.axis_index("xy")
    greet(count, me)
    copies = []
    for step in range(1, count):
        copy = pltpu.make_async_remote_copy(
            src_ref=source,
            dst_ref=out.at[me],
            send_sem=send_sems.at[step - 1],
            recv_sem=recv_sems.at[step - 1],
            device_id={"xy": lax.rem(me + step, count)},
            device_id_type=pl.DeviceIdType.MESH,
        )
        copy.start()
        copies.append(copy)
    out[me] = source[...]
    for copy in copies:
        copy.wait()


def gathered(value, count, number):
    sems = pltpu.SemaphoreType.DMA((count - 1,))
    return pl.pallas_call(
        functools.partial(gather_kernel, count),
        out_shape=jax.ShapeDtypeStruct((count,) + value.shape, jnp.float32),
        in_specs=[in_vmem],
        out_specs=in_vmem,
        scratch_shapes=[sems, sems],
        compiler_params=pltpu.CompilerParams(collective_id=number, has_side_effects=True),
    )(value)


def local(
    electric, magnetic_first, magnetic_second, region, permittivity_table, conductivity_table
):
    count = lax.axis_size("xy")
    me = lax.axis_index("xy")
    _, rows, columns = electric.shape
    width = columns // count
    pieces = 2 if rows % 256 == 0 else 1
    parts = 1
    piece_rows = rows // pieces
    part_columns = columns // parts
    runs = 8
    electric, hx, hy, region = (
        v.reshape(rows, columns) for v in (electric, magnetic_first, magnetic_second, region)
    )
    eps, sig = permittivity_table, conductivity_table
    first_flag = (me == 0).astype(jnp.int32).reshape(1)
    me_value = me.astype(jnp.int32).reshape(1)

    cut = [slice(p * piece_rows, (p + 1) * piece_rows) for p in range(pieces)]
    ups = [passed_along(electric[c], "gz", 1) for c in cut]
    downs = [passed_along(electric[c], "gz", -1) for c in cut]
    hx_edge = passed_along(hx[-1:], "xy", 1)
    e_before = passed_along(electric[-1:], "xy", 1)
    e_after = passed_along(electric[:1], "xy", -1)

    halves = []
    lines = max(piece_rows, 128)
    t_shape = (columns, lines)
    for p in range(pieces):
        edge = hx_edge if p == 0 else hx[p * piece_rows - 1:p * piece_rows]
        halves.append(called(
            functools.partial(x_kernel, parts),
            [(piece_rows, part_columns)] * parts,
            [(lines, columns)] * 2 + [t_shape] * 2 + [((run_length - 1) * columns // run_length, lines)] * 3,
            [in_vmem] * 7 + [in_smem] * 2,
            piece_rows * columns,
            (electric[cut[p]], ups[p], downs[p], hx[cut[p]], edge, hy[cut[p]], region[cut[p]],
             eps, sig),
        ))
    half_up = [[passed_along(halves[p][c], "gz", 1) for p in range(pieces)] for c in range(parts)]
    half_down = [
        [passed_along(halves[p][c], "gz", -1) for p in range(pieces)] for c in range(parts)
    ]
    middle = called(
        functools.partial(middle_kernel, parts, pieces),
        [(rows, part_columns)] * parts
        + [(part_columns // 128, rows, 128)] * parts
        + [(rows, part_columns)] * parts
        + [(columns, rows)],
        [(rows, columns)] * 2,
        [in_smem] + [in_vmem] * 7 + [in_smem] * 2 + [in_vmem] * (parts * pieces),
        rows * columns,
        (first_flag, electric, hx, hy, region, e_before, e_after, hx_edge, eps, sig,
         *[halves[p][c] for p in range(pieces) for c in range(parts)]),
    )
    right_sides, diagonals = middle[:parts], middle[parts:2 * parts]
    half_hx, full_hy_t = middle[2 * parts:3 * parts], middle[3 * parts]

    def exchanged(values, size):
        moved = lax.all_to_all(
            values.reshape(count, size, rows), "xy", split_axis=0, concat_axis=0, tiled=True
        )
        return moved

    def joined(moved):
        return jnp.transpose(moved, (1, 0, 2)).reshape(1, moved.shape[1], count * rows)

    by_kernel = rows % 128 == 0 and width % 8 == 0 and 1 < count <= 16
    if by_kernel:
        full_hy, = spread([full_hy_t], count, 0)
        full_hy, right_side = lax.optimization_barrier((full_hy, right_sides[0]))
    else:
        full_hy, right_side = joined(exchanged(full_hy_t, width)), right_sides[0]
    length = rows // runs
    kept = ((length - 1) * runs, columns)
    firsts = called(
        functools.partial(y_first_kernel, pieces, runs),
        [kept] * 3 + [(3 * runs, columns), (8, columns)],
        [(columns // 128, rows, 128)],
        [in_vmem] * (2 + 2 * pieces),
        rows * columns,
        (right_side, diagonals[0], *half_up[0], *half_down[0]),
    )
    everyone = gathered(firsts[4], count, 1) if by_kernel else lax.all_gather(firsts[4], "xy")
    seconds = called(
        functools.partial(y_second_kernel, count, runs),
        [(columns, rows)] * 2,
        [(columns // 128, rows, 128), (rows, columns), (runs, columns)],
        [in_smem] + [in_vmem] * 6,
        rows * columns,
        (me_value, jnp.swapaxes(everyone, 0, 1), *firsts[:4], half_hx[0]),
    )
    if by_kernel:
        full_e, full_hx = spread(seconds, count, 2)
    else:
        full_e, full_hx = (joined(exchanged(v, width)) for v in seconds)
    return tuple(v.reshape(1, width, count * rows) for v in (full_e, full_hx, full_hy))


def solution(mesh):
    in_specs = (
        P("gz", "xy", None),
        P("gz", "xy", None),
        P("gz", "xy", None),
        P("gz", "xy", None),
        P(),
        P(),
    )
    out_specs = (P("gz", "xy", None), P("gz", "xy", None), P("gz", "xy", None))
    return jax.shard_map(local, mesh=mesh, in_specs=in_specs, out_specs=out_specs, check_vma=False)
```
